256 devices in a mesh: dp: 32 (over z, y), tensor: 8 (over x, core).
Axes of the slice: x: 4, y: 4, z: 8, core: 2. Of those that a mesh axis runs over, the one named last changes fastest.
Arguments:
- tokens: bfloat16 [2, 512, 12288], P(None, 'dp', 'tensor'), may hold values from -6 to 6
- up_weight: bfloat16 [12288, 49152], P('tensor', 'dp'), may hold values from -0.0546875 to 0.0546875
- up_bias: bfloat16 [49152], P('dp'), may hold values from -3 to 3
- down_weight: bfloat16 [49152, 12288], P('dp', 'tensor'), may hold values from -0.02734375 to 0.02734375
- down_bias: bfloat16 [12288], P('tensor'), may hold values from -3 to 3
- active: int32 [2, 4, 384], P(None, None, 'dp'), may hold values from 0 to 1
Outputs:
- mixed: bfloat16 [2, 512, 12288], P(None, 'dp', 'tensor')
The draws below stay inside these ranges and needn't reach their ends.
All inputs are finite; a program needn't handle non-finite values.
Results may differ from the reference program's by a relative error of at most 0.0042.
Values may be sent and summed in bfloat16 or wider, within the bound.
No kernel may reach another device: no remote copies, remote signals or barrier semaphores. Data moves between devices by JAX's collectives and lax.ppermute only.
A program may use at most 64 MiB of HBM per device.

```python
import jax
import jax.numpy as jnp

D = 12288
FF = 49152
HBLK = 128
RBLK = 128
STEPS = 2
ROWS = 512


def draw_active(key, part):
    groups = FF // HBLK // 4
    levels = jax.random.randint(jax.random.fold_in(key, 11), (groups,), 1, 8)
    coins = jax.random.randint(jax.random.fold_in(key, 12), (STEPS, ROWS // RBLK, FF // HBLK), 0, 8)
    return (coins < jnp.repeat(levels, 4)[None, None, :]).astype(jnp.int32)


def shard_levels(rng, extent, pieces, low, high):
    loudness = 1.0
    for position, parts in pieces:
        heights = jax.random.uniform(jax.random.fold_in(jax.random.fold_in(rng, 6), position), (parts,), jnp.float32, low / len(pieces), high / len(pieces))
        loudness = loudness * jnp.repeat(jnp.exp(heights), extent[position] // parts).reshape((-1,) + (1,) * (len(extent) - 1 - position))
    return loudness


def gaussian(key, dims, spread, reach, cuts=(), held_as=jnp.bfloat16):
    result = jax.random.normal(key, dims, jnp.float32) * spread
    if len(cuts) > 0:
        result = shard_levels(key, dims, cuts, -0.22, 0.18) * result
    return jnp.clip(result, min=-reach, max=reach).astype(held_as)


def setup_inputs(seed: int = 0) -> dict:
    splits = jax.random.split(jax.random.key(seed), 7)
    tokens = gaussian(splits[0], (STEPS, ROWS, D), 1.0, 6.0, ((1, 32), (2, 8)))
    up_weight = gaussian(splits[1], (D, FF), D ** -0.5, 0.0546875, ((0, 8), (1, 32)))
    up_bias = gaussian(splits[2], (FF,), 0.5, 3.0, ((0, 32),))
    down_weight = gaussian(splits[3], (FF, D), FF ** -0.5, 0.02734375, ((0, 32), (1, 8)))
    down_bias = gaussian(splits[4], (D,), 0.5, 3.0, ((0, 8),))
    active = draw_active(jax.random.fold_in(splits[6], 71), 0)
    return {"tokens": tokens, "up_weight": up_weight, "up_bias": up_bias, "down_weight": down_weight, "down_bias": down_bias, "active": active}


def reference(tokens, up_weight, up_bias, down_weight, down_bias, active):
    results = []
    for step_index in range(STEPS):
        preact = jnp.dot(tokens[step_index], up_weight, preferred_element_type=jnp.float32) + up_bias.astype(jnp.float32)
        row_mask = jnp.repeat(jnp.repeat(active[step_index].astype(jnp.float32), RBLK, axis=0), HBLK, axis=1)
        hidden = (jnp.maximum(preact, 0.0) * row_mask).astype(jnp.bfloat16)
        summed = jnp.dot(hidden, down_weight, preferred_element_type=jnp.float32) + down_bias.astype(jnp.float32)
        results.append(summed.astype(jnp.bfloat16))
    return jnp.stack(results)
```

```python
import jax
import jax.numpy as jnp
from jax import lax
from jax.sharding import PartitionSpec as P

AXES = ("dp", "tensor")
NZ, NY, NX, NC = 8, 4, 4, 2
F32 = jnp.float32
BF16 = jnp.bfloat16


def shift(value, dz=0, dy=0, dx=0, dc=0):
    pairs = []
    for z in range(NZ):
        for y in range(NY):
            for x in range(NX):
                for c in range(NC):
                    source = ((z * NY + y) * NX + x) * NC + c
                    zt, yt, xt, ct = (z + dz) % NZ, (y + dy) % NY, (x + dx) % NX, (c + dc) % NC
                    pairs.append((source, ((zt * NY + yt) * NX + xt) * NC + ct))
    return lax.ppermute(value, AXES, pairs)


Z_SLOTS = (0, 1, -1, 2, -2, 3, 4, -3)
Y_SLOTS = (0, 1, -1, 2)


def gather_z(block):
    p1, m1 = shift(block, dz=1), shift(block, dz=-1)
    p2, m2 = shift(block, dz=2), shift(block, dz=-2)
    far = shift(jnp.concatenate([p1, p2]), dz=2)
    back = shift(m1, dz=-2)
    return jnp.concatenate([block, p1, m1, p2, m2, far, back])


def scatter_z(sums):
    far = shift(sums[5:7].astype(BF16), dz=-2).astype(F32)
    back = shift(sums[7:8].astype(BF16), dz=2).astype(F32)
    p1 = (sums[1] + far[0]).astype(BF16)
    p2 = (sums[3] + far[1]).astype(BF16)
    m1 = (sums[2] + back[0]).astype(BF16)
    m2 = sums[4].astype(BF16)
    return (
        sums[0]
        + shift(p1, dz=-1).astype(F32)
        + shift(m1, dz=1).astype(F32)
        + shift(p2, dz=-2).astype(F32)
        + shift(m2, dz=2).astype(F32)
    )


def local(tokens, up_weight, up_bias, down_weight, down_bias, active):
    steps, rows, width = tokens.shape
    hidden_width = up_weight.shape[1]
    blocks = active.shape[2]
    z = lax.axis_index("dp") // NY
    x = lax.axis_index("tensor") // NC
    c = lax.axis_index("tensor") % NC
    own = steps * rows
    slot = NZ * own
    half = NY * slot // NC
    piece = half // NX

    column = gather_z(tokens.reshape(own, width))
    gathered = jnp.concatenate([column] + [shift(column, dy=k) for k in Y_SLOTS[1:]])

    def project(start):
        part = lax.dynamic_slice_in_dim(gathered, start, half)
        return jnp.dot(part, up_weight, preferred_element_type=F32)

    away = shift(project((1 - c) * half).astype(BF16), dc=1)
    sums = project(c * half) + away.astype(F32)

    def piece_for(k):
        return lax.dynamic_slice_in_dim(sums, ((x + k) % NX) * piece, piece)

    total = piece_for(0)
    for k in (1, -1, 2):
        total = total + shift(piece_for(k).astype(BF16), dx=k).astype(F32)

    z_slots = jnp.asarray(Z_SLOTS, jnp.int32).reshape(2, 4)[x % 2]
    row_block = ((z - z_slots) % NZ) // 2
    mask = jnp.swapaxes(jnp.take(active, row_block, axis=1), 0, 1)
    mask = mask.astype(F32)[:, :, None, :, None]
    preact = jnp.maximum(total + up_bias.astype(F32), 0.0)
    gated = preact.reshape(4, steps, rows, blocks, hidden_width // blocks) * mask
    mine = gated.reshape(piece, hidden_width).astype(BF16)

    near = jnp.zeros((half, hidden_width), BF16)
    near = lax.dynamic_update_slice_in_dim(near, mine, x * piece, 0)
    for k in (1, -1, 2):
        near = lax.dynamic_update_slice_in_dim(near, shift(mine, dx=k), ((x - k) % NX) * piece, 0)
    other = shift(near, dc=1)
    hidden = jnp.concatenate([jnp.where(c == 0, near, other), jnp.where(c == 0, other, near)])

    outs = [
        jnp.dot(hidden[i * slot : (i + 1) * slot], down_weight, preferred_element_type=F32)
        for i in range(NY)
    ]
    scattered = outs[0]
    for i in (1, 2, 3):
        scattered = scattered + shift(outs[i].astype(BF16), dy=-Y_SLOTS[i]).astype(F32)
    mixed = scatter_z(scattered.reshape(NZ, own, width)) + down_bias.astype(F32)
    return mixed.astype(BF16).reshape(steps, rows, width)


def solution(mesh):
    placed = (
        P(None, "dp", "tensor"),
        P("tensor", "dp"),
        P("dp"),
        P("dp", "tensor"),
        P("tensor"),
        P(None, None, "dp"),
    )
    return jax.shard_map(
        local, mesh=mesh, in_specs=placed, out_specs=P(None, "dp", "tensor"), check_vma=False
    )
```

```python
import jax
import jax.numpy as jnp
from jax import lax
from jax.experimental import pallas as pl
from jax.experimental.pallas import tpu as pltpu
from jax.sharding import PartitionSpec as P

AXES = ("dp", "tensor")
NZ, NY, NX, NC = 8, 4, 4, 2
Z_GROUPS = [[z * NY + y for z in range(NZ)] for y in range(NY)]
F32 = jnp.float32
BF16 = jnp.bfloat16
TILE = 256
VMEM = pl.BlockSpec(memory_space=pltpu.VMEM)


def shift(value, dz=0, dy=0, dx=0, dc=0):
    pairs = []
    for z in range(NZ):
        for y in range(NY):
            for x in range(NX):
                for c in range(NC):
                    source = ((z * NY + y) * NX + x) * NC + c
                    zt, yt, xt, ct = (z + dz) % NZ, (y + dy) % NY, (x + dx) % NX, (c + dc) % NC
                    pairs.append((source, ((zt * NY + yt) * NX + xt) * NC + ct))
    return lax.ppermute(value, AXES, pairs)


def exchange_z(blocks):
    return lax.all_to_all(blocks, "dp", 0, 0, tiled=True, axis_index_groups=Z_GROUPS)


def gather_z(block):
    copies = jnp.broadcast_to(block[None], (NZ,) + block.shape)
    return exchange_z(copies).reshape(NZ * block.shape[0], block.shape[1])


def up_kernel(col, prev, succ, far, weight, own, away, held):
    c = lax.axis_index("tensor") % NC
    j = pl.program_id(0)
    slot = col.shape[0]
    half = own.shape[0]

    @pl.when(j == 0)
    def _():
        near_at = pl.multiple_of(c * half, half)
        far_at = pl.multiple_of((1 - c) * half, half)
        held[pl.ds(near_at, slot), :] = col[...]
        held[pl.ds(near_at + slot, slot), :] = prev[...]
        held[pl.ds(far_at, slot), :] = succ[...]
        held[pl.ds(far_at + slot, slot), :] = far[...]

    columns = pl.ds(pl.multiple_of(j * TILE, TILE), TILE)
    product = jnp.dot(held[...], weight[...], preferred_element_type=F32)
    own[:, columns] = product[:half]
    away[:, columns] = product[half:].astype(BF16)


def up(col, prev, succ, far, weight):
    slot, depth = col.shape
    width = weight.shape[1]
    half = 2 * slot
    return pl.pallas_call(
        up_kernel,
        grid=(width // TILE,),
        in_specs=[VMEM] * 4 + [pl.BlockSpec((depth, TILE), lambda j: (0, j))],
        out_specs=[VMEM] * 2,
        out_shape=[
            jax.ShapeDtypeStruct((half, width), F32),
            jax.ShapeDtypeStruct((half, width), BF16),
        ],
        scratch_shapes=[pltpu.VMEM((2 * half, depth), BF16)],
        compiler_params=pltpu.CompilerParams(vmem_limit_bytes=24 * 2**20),
        cost_estimate=pl.CostEstimate(
            flops=4 * half * depth * width, bytes_accessed=2 * depth * width, transcendentals=0
        ),
    )(col, prev, succ, far, weight)


def down_kernel(near, other, weight, out0, out1, out2, out3, held):
    c = lax.axis_index("tensor") % NC
    j = pl.program_id(0)
    half = near.shape[0]
    slot = out0.shape[0]

    @pl.when(j == 0)
    def _():
        held[pl.ds(pl.multiple_of(c * half, half), half), :] = near[...]
        held[pl.ds(pl.multiple_of((1 - c) * half, half), half), :] = other[...]

    columns = pl.ds(pl.multiple_of(j * TILE, TILE), TILE)
    product = jnp.dot(held[...], weight[...], preferred_element_type=F32)
    out0[:, columns] = product[:slot]
    out1[:, columns] = product[slot : 2 * slot].astype(BF16)
    out2[:, columns] = product[2 * slot : 3 * slot].astype(BF16)
    out3[:, columns] = product[3 * slot :].astype(BF16)


def down(near, other, weight):
    half, depth = near.shape
    width = weight.shape[1]
    slot = half // 2
    return pl.pallas_call(
        down_kernel,
        grid=(width // TILE,),
        in_specs=[VMEM] * 2 + [pl.BlockSpec((depth, TILE), lambda j: (0, j))],
        out_specs=[VMEM] * 4,
        out_shape=[jax.ShapeDtypeStruct((slot, width), F32)]
        + [jax.ShapeDtypeStruct((slot, width), BF16)] * 3,
        scratch_shapes=[pltpu.VMEM((2 * half, depth), BF16)],
        compiler_params=pltpu.CompilerParams(vmem_limit_bytes=24 * 2**20),
        cost_estimate=pl.CostEstimate(
            flops=4 * half * depth * width, bytes_accessed=2 * depth * width, transcendentals=0
        ),
    )(near, other, weight)


def local(tokens, up_weight, up_bias, down_weight, down_bias, active):
    steps, rows, width = tokens.shape
    hidden_width = up_weight.shape[1]
    blocks = active.shape[2]
    x = lax.axis_index("tensor") // NC
    slot = NZ * rows
    half = 2 * slot
    piece = half // NX
    up_bias = up_bias.astype(F32)
    down_bias = down_bias.astype(F32)

    opposite = shift(tokens.reshape(steps * rows, width), dy=2).reshape(tokens.shape)

    def start_rows(own):
        col = gather_z(own)
        return col, shift(col, dy=1), shift(col, dy=-1)

    def start_sums(col, prev, succ, far):
        own, away = up(col, prev, succ, far, up_weight)
        away = shift(away, dc=1)

        def piece_for(k):
            at = ((x + k) % NX) * piece
            return lax.dynamic_slice_in_dim(own, at, piece) + lax.dynamic_slice_in_dim(
                away, at, piece
            ).astype(F32)

        return piece_for(0), [piece_for(k).astype(BF16) for k in (1, -1, 2)]

    def activate(total, arrived, step):
        for part in arrived:
            total = total + part.astype(F32)
        mask = lax.dynamic_slice_in_dim(active[step], (x % 2) * 2, 2).astype(F32)
        preact = jnp.maximum(total + up_bias, 0.0)
        gated = preact.reshape(2, piece // 2, blocks, -1) * mask[:, None, :, None]
        return gated.reshape(piece, hidden_width).astype(BF16)

    def send_x(parts):
        return [shift(part, dx=k) for part, k in zip(parts, (1, -1, 2))]

    def combine_x(mine, arrived):
        near = jnp.zeros((half, hidden_width), BF16)
        near = lax.dynamic_update_slice_in_dim(near, mine, x * piece, 0)
        for part, k in zip(arrived, (1, -1, 2)):
            near = lax.dynamic_update_slice_in_dim(near, part, ((x - k) % NX) * piece, 0)
        return down(near, shift(near, dc=1), down_weight)

    def sum_z(part):
        return exchange_z(part.reshape(NZ, rows, width)).astype(F32).sum(0)

    col0, prev0, succ0 = start_rows(tokens[0])
    far0 = gather_z(opposite[0])
    total0, parts0 = start_sums(col0, prev0, succ0, far0)
    parts0, own1 = lax.optimization_barrier((parts0, tokens[1]))
    arrived0 = send_x(parts0)
    col1, prev1, succ1 = start_rows(own1)
    mine0 = activate(total0, arrived0, 0)
    mine0, opposite1 = lax.optimization_barrier((mine0, opposite[1]))
    hidden0 = send_x([mine0] * 3)
    far1 = gather_z(opposite1)
    outs0 = combine_x(mine0, hidden0)
    total1, parts1 = start_sums(col1, prev1, succ1, far1)
    parts1, outs0 = lax.optimization_barrier((parts1, outs0))
    arrived1 = send_x(parts1)
    back0 = [shift(outs0[1], dy=-1), shift(outs0[2], dy=1)]
    opposite0 = sum_z(outs0[3])
    mine1 = activate(total1, arrived1, 1)
    sent0 = (outs0[0] + back0[0].astype(F32) + back0[1].astype(F32)).astype(BF16)
    mine1, sent0, opposite0 = lax.optimization_barrier((mine1, sent0, opposite0))
    hidden1 = send_x([mine1] * 3)
    crossed0 = shift(opposite0.astype(BF16), dy=2)
    mixed0 = sum_z(sent0) + crossed0.astype(F32) + down_bias
    outs1 = combine_x(mine1, hidden1)
    back1 = [shift(outs1[1], dy=-1), shift(outs1[2], dy=1)]
    opposite1 = sum_z(outs1[3])
    sent1 = (outs1[0] + back1[0].astype(F32) + back1[1].astype(F32)).astype(BF16)
    sent1, opposite1 = lax.optimization_barrier((sent1, opposite1))
    crossed1 = shift(opposite1.astype(BF16), dy=2)
    mixed1 = sum_z(sent1) + crossed1.astype(F32) + down_bias
    return jnp.stack([mixed0.astype(BF16), mixed1.astype(BF16)])


def solution(mesh):
    placed = (
        P(None, "dp", "tensor"),
        P("tensor", "dp"),
        P("dp"),
        P("dp", "tensor"),
        P("tensor"),
        P(None, None, "dp"),
    )
    return jax.shard_map(
        local, mesh=mesh, in_specs=placed, out_specs=P(None, "dp", "tensor"), check_vma=False
    )
```

```python
import jax
import jax.numpy as jnp
from jax import lax
from jax.experimental import pallas as pl
from jax.experimental.pallas import tpu as pltpu
from jax.sharding import PartitionSpec as P

AXES = ("dp", "tensor")
NZ, NY, NX, NC = 8, 4, 4, 2
Z_GROUPS = [[z * NY + y for z in range(NZ)] for y in range(NY)]
F32 = jnp.float32
BF16 = jnp.bfloat16
TILE = 256


def shift(value, dz=0, dy=0, dx=0, dc=0):
    pairs = []
    for z in range(NZ):
        for y in range(NY):
            for x in range(NX):
                for c in range(NC):
                    source = ((z * NY + y) * NX + x) * NC + c
                    zt, yt, xt, ct = (z + dz) % NZ, (y + dy) % NY, (x + dx) % NX, (c + dc) % NC
                    pairs.append((source, ((zt * NY + yt) * NX + xt) * NC + ct))
    return lax.ppermute(value, AXES, pairs)


def exchange_z(blocks):
    return lax.all_to_all(blocks, "dp", 0, 0, tiled=True, axis_index_groups=Z_GROUPS)


def gather_z(block):
    copies = jnp.broadcast_to(block[None], (NZ,) + block.shape)
    return exchange_z(copies).reshape(NZ * block.shape[0], block.shape[1])


def up_kernel(col, prev, succ, far, weight, own, away):
    rows = own.shape[1] // NZ
    for i, slot in enumerate((col, prev, succ, far)):
        product = jnp.dot(slot[...], weight[...], preferred_element_type=F32)
        for z in range(NZ):
            at = 2 * z * rows
            own[i, z * rows : (z + 1) * rows] = product[at : at + rows]
            away[i, z * rows : (z + 1) * rows] = product[at + rows : at + 2 * rows].astype(BF16)


def up(slots, weight):
    size, depth = slots[0].shape
    width = weight.shape[1]
    shape = (NY, size // 2, width)
    return pl.pallas_call(
        up_kernel,
        grid=(width // TILE,),
        in_specs=[pl.BlockSpec((size, depth), lambda j: (0, 0))] * 4
        + [pl.BlockSpec((depth, TILE), lambda j: (0, j))],
        out_specs=[pl.BlockSpec((NY, size // 2, TILE), lambda j: (0, 0, j))] * 2,
        out_shape=[jax.ShapeDtypeStruct(shape, F32), jax.ShapeDtypeStruct(shape, BF16)],
        compiler_params=pltpu.CompilerParams(vmem_limit_bytes=58 * 2**20),
        cost_estimate=pl.CostEstimate(
            flops=8 * size * depth * width, bytes_accessed=2 * depth * width, transcendentals=0
        ),
    )(*slots, weight)


def down_kernel(near, other, weight, *outs):
    size = near.shape[1]
    rows = size // NZ
    for t, source in enumerate((near, other)):
        hidden = source[...].reshape(NY * size, source.shape[2])
        product = jnp.dot(hidden, weight[...], preferred_element_type=F32)
        for i, out in enumerate(outs):
            for z in range(NZ):
                at = i * size + z * rows
                to = (2 * z + t) * rows
                out[to : to + rows] = product[at : at + rows].astype(out.dtype)


def down(near, other, weight):
    _, size, depth = near.shape
    width = weight.shape[1]
    return pl.pallas_call(
        down_kernel,
        grid=(width // TILE,),
        in_specs=[pl.BlockSpec((NY, size, depth), lambda j: (0, 0, 0))] * 2
        + [pl.BlockSpec((depth, TILE), lambda j: (0, j))],
        out_specs=[pl.BlockSpec((2 * size, TILE), lambda j: (0, j))] * 4,
        out_shape=[jax.ShapeDtypeStruct((2 * size, width), F32)]
        + [jax.ShapeDtypeStruct((2 * size, width), BF16)] * 3,
        compiler_params=pltpu.CompilerParams(vmem_limit_bytes=58 * 2**20),
        cost_estimate=pl.CostEstimate(
            flops=16 * size * depth * width, bytes_accessed=2 * depth * width, transcendentals=0
        ),
    )(near, other, weight)


def local(tokens, up_weight, up_bias, down_weight, down_bias, active):
    steps, rows, width = tokens.shape
    hidden_width = up_weight.shape[1]
    blocks = active.shape[2]
    x = lax.axis_index("tensor") // NC
    c = lax.axis_index("tensor") % NC
    up_bias = up_bias.astype(F32)
    down_bias = down_bias.astype(F32)

    own = jnp.where(c == 0, tokens, tokens[::-1]).reshape(steps * rows, width)
    opposite = shift(own, dy=2)
    col = gather_z(own)
    prev, succ = shift(col, dy=1), shift(col, dy=-1)
    far = gather_z(opposite)

    mine, away = up((col, prev, succ, far), up_weight)
    away = shift(away, dc=1)

    def slot_for(k):
        at = (x + k) % NX
        return mine[at] + away[at].astype(F32)

    sends = (1, -1, 2)
    total = slot_for(0)
    for k in sends:
        total = total + shift(slot_for(k).astype(BF16), dx=k).astype(F32)
    mask = jnp.repeat(active[c].astype(F32), 2, axis=0)
    preact = jnp.maximum(total + up_bias, 0.0)
    gated = preact.reshape(NZ, rows, blocks, -1) * mask[:, None, :, None]
    gated = gated.reshape(NZ * rows, hidden_width).astype(BF16)

    near = jnp.zeros((NX,) + gated.shape, BF16)
    near = lax.dynamic_update_index_in_dim(near, gated, x, 0)
    for k in sends:
        near = lax.dynamic_update_index_in_dim(near, shift(gated, dx=k), (x - k) % NX, 0)
    outs = down(near, shift(near, dc=1), down_weight)

    def sum_z(part):
        return exchange_z(part.reshape(NZ, steps * rows, width)).astype(F32).sum(0)

    back = [shift(outs[1], dy=-1), shift(outs[2], dy=1)]
    crossed = shift(sum_z(outs[3]).astype(BF16), dy=2)
    summed = outs[0] + back[0].astype(F32) + back[1].astype(F32)
    mixed = (sum_z(summed.astype(BF16)) + crossed.astype(F32) + down_bias).astype(BF16)
    mixed = mixed.reshape(tokens.shape)
    return jnp.where(c == 0, mixed, mixed[::-1])


def solution(mesh):
    placed = (
        P(None, "dp", "tensor"),
        P("tensor", "dp"),
        P("dp"),
        P("dp", "tensor"),
        P("tensor"),
        P(None, None, "dp"),
    )
    return jax.shard_map(
        local, mesh=mesh, in_specs=placed, out_specs=P(None, "dp", "tensor"), check_vma=False
    )
```

```python
import jax
import jax.numpy as jnp
from jax import lax
from jax.sharding import PartitionSpec as P

AXES = ("dp", "tensor")
NZ, NY, NX, NC = 8, 4, 4, 2
F32 = jnp.float32
BF16 = jnp.bfloat16


def shift(value, dz=0, dy=0, dx=0, dc=0):
    pairs = []
    for z in range(NZ):
        for y in range(NY):
            for x in range(NX):
                for c in range(NC):
                    source = ((z * NY + y) * NX + x) * NC + c
                    zt, yt, xt, ct = (z + dz) % NZ, (y + dy) % NY, (x + dx) % NX, (c + dc) % NC
                    pairs.append((source, ((zt * NY + yt) * NX + xt) * NC + ct))
    return lax.ppermute(value, AXES, pairs)


Z_BLOCKS = (0, 1, 2, 3, 4, -1, -2, -3)


def gather_z(block):
    ahead, behind = [block], [block]
    for step in range(4):
        ahead.append(shift(ahead[-1], dz=1))
        if step < 3:
            behind.append(shift(behind[-1], dz=-1))
    return jnp.concatenate(ahead + behind[1:])


def scatter_z(sums):
    back, forth = sums[4], sums[7]
    for step in range(4):
        back = sums[3 - step] + shift(back.astype(BF16), dz=-1).astype(F32)
        if step < 2:
            forth = sums[6 - step] + shift(forth.astype(BF16), dz=1).astype(F32)
    return back + shift(forth.astype(BF16), dz=1).astype(F32)


def local(tokens, up_weight, up_bias, down_weight, down_bias, active):
    steps, rows, width = tokens.shape
    hidden_width = up_weight.shape[1]
    blocks = active.shape[2]
    z = lax.axis_index("dp") // NY
    x = lax.axis_index("tensor") // NC
    c = lax.axis_index("tensor") % NC
    up_bias = up_bias.astype(F32)
    down_bias = down_bias.astype(F32)

    own = jnp.where(c == 0, tokens, tokens[::-1]).reshape(steps * rows, width)
    opposite = shift(own, dy=2)
    col = gather_z(own)
    prev, succ = shift(col, dy=1), shift(col, dy=-1)
    opposite, col = lax.optimization_barrier((opposite, col))
    far = gather_z(opposite)

    products = [
        jnp.dot(slot, up_weight, preferred_element_type=F32).reshape(NZ, steps, rows, hidden_width)
        for slot in (col, prev, succ, far)
    ]
    mine = [product[:, 0].reshape(NZ * rows, hidden_width) for product in products]
    away = [product[:, 1].reshape(NZ * rows, hidden_width).astype(BF16) for product in products]
    first = shift(away[0], dc=1)
    rest = shift(jnp.stack(away[1:]), dc=1)
    sums = jnp.stack(
        [mine[0] + first.astype(F32)] + [mine[i] + rest[i - 1].astype(F32) for i in (1, 2, 3)]
    )

    def slot_for(k):
        return sums[(x + k) % NX]

    sends = (1, -1, 2)
    total = slot_for(0)
    for k in sends:
        total = total + shift(slot_for(k).astype(BF16), dx=k).astype(F32)
    row_block = ((z - jnp.asarray(Z_BLOCKS, jnp.int32)) % NZ) // 2
    mask = active[c][row_block].astype(F32)
    preact = jnp.maximum(total + up_bias, 0.0)
    gated = preact.reshape(NZ, rows, blocks, -1) * mask[:, None, :, None]
    gated = gated.reshape(NZ * rows, hidden_width).astype(BF16)

    near = jnp.zeros((NX,) + gated.shape, BF16)
    near = lax.dynamic_update_index_in_dim(near, gated, x, 0)
    for k in sends:
        near = lax.dynamic_update_index_in_dim(near, shift(gated, dx=k), (x - k) % NX, 0)
    other = shift(near, dc=1)

    def out(i):
        pair = [part[i].reshape(NZ, 1, rows, hidden_width) for part in (near, other)]
        hidden = jnp.concatenate(pair, 1).reshape(NZ * steps * rows, hidden_width)
        return jnp.dot(hidden, down_weight, preferred_element_type=F32)

    back = [shift(out(1).astype(BF16), dy=-1), shift(out(2).astype(BF16), dy=1)]

    def sum_z(part):
        return scatter_z(part.reshape(NZ, steps * rows, width))

    crossed = shift(sum_z(out(3)).astype(BF16), dy=2)
    summed = out(0) + back[0].astype(F32) + back[1].astype(F32)
    mixed = (sum_z(summed) + crossed.astype(F32) + down_bias).astype(BF16)
    mixed = mixed.reshape(tokens.shape)
    return jnp.where(c == 0, mixed, mixed[::-1])


def solution(mesh):
    placed = (
        P(None, "dp", "tensor"),
        P("tensor", "dp"),
        P("dp"),
        P("dp", "tensor"),
        P("tensor"),
        P(None, None, "dp"),
    )
    return jax.shard_map(
        local, mesh=mesh, in_specs=placed, out_specs=P(None, "dp", "tensor"), check_vma=False
    )
```

```python
import jax
import jax.numpy as jnp
from jax import lax
from jax.sharding import PartitionSpec as P

AXES = ("dp", "tensor")
NZ, NY, NX, NC = 8, 4, 4, 2
F32 = jnp.float32
BF16 = jnp.bfloat16


def shift(value, dz=0, dy=0, dx=0, dc=0):
    pairs = []
    for z in range(NZ):
        for y in range(NY):
            for x in range(NX):
                for c in range(NC):
                    source = ((z * NY + y) * NX + x) * NC + c
                    zt, yt, xt, ct = (z + dz) % NZ, (y + dy) % NY, (x + dx) % NX, (c + dc) % NC
                    pairs.append((source, ((zt * NY + yt) * NX + xt) * NC + ct))
    return lax.ppermute(value, AXES, pairs)


Z_BLOCKS = (0, 1, -1, 2, -2, 3, -3, 4)


def gather_z(block):
    held = {0: block}
    for k in (1, 2, 3, 4):
        held[k] = shift(held[k - 1], dz=1)
        if k < 4:
            held[-k] = shift(held[1 - k], dz=-1)
    return [held[k] for k in Z_BLOCKS]


def scatter_z(sums):
    part = dict(zip(Z_BLOCKS, sums))
    back, forth = part[4], part[-3]
    for k in (3, 2, 1):
        back = part[k] + shift(back.astype(BF16), dz=-1).astype(F32)
        if k < 3:
            forth = part[-k] + shift(forth.astype(BF16), dz=1).astype(F32)
    return part[0] + shift(back, dz=-1) + shift(forth, dz=1)


def local(tokens, up_weight, up_bias, down_weight, down_bias, active):
    steps, rows, width = tokens.shape
    own_rows = steps * rows
    slot = NZ * own_rows
    hidden_width = up_weight.shape[1]
    columns = hidden_width // NC
    blocks = active.shape[2] // NC
    z = lax.axis_index("dp") // NY
    x = lax.axis_index("tensor") // NC
    c = lax.axis_index("tensor") % NC

    up_own, up_away, down_own, down_away = lax.optimization_barrier((
        lax.dynamic_slice_in_dim(up_weight, c * columns, columns, 1),
        lax.dynamic_slice_in_dim(up_weight, (1 - c) * columns, columns, 1),
        lax.dynamic_slice_in_dim(down_weight, c * columns, columns, 0),
        lax.dynamic_slice_in_dim(down_weight, (1 - c) * columns, columns, 0),
    ))
    up_bias = lax.dynamic_slice_in_dim(up_bias, c * columns, columns).astype(F32)
    active = lax.dynamic_slice_in_dim(active, c * blocks, blocks, 2).astype(F32)
    row_block = ((z - jnp.asarray(Z_BLOCKS, jnp.int32)) % NZ) // 2
    chosen = (row_block[:, None] == jnp.arange(active.shape[1], dtype=jnp.int32)[None]).astype(F32)
    mask = (chosen[:, None, :, None] * active[None]).sum(2)

    own = tokens.reshape(own_rows, width)
    opposite = shift(own, dy=2)
    col = gather_z(own)
    halves = [jnp.concatenate(col[:4]), jnp.concatenate(col[4:])]
    prev = jnp.concatenate([shift(half, dy=1) for half in halves])
    succ = jnp.concatenate([shift(half, dy=-1) for half in halves])
    far = jnp.concatenate(gather_z(opposite))
    slots = (jnp.concatenate(halves), prev, succ, far)

    away = [shift(jnp.dot(part, up_away, preferred_element_type=F32), dc=1) for part in slots]
    mine = [jnp.dot(part, up_own, preferred_element_type=F32) for part in slots]
    sums = jnp.stack([a + b for a, b in zip(mine, away)])

    def slot_for(k):
        return sums[(x + k) % NX]

    sends = (1, -1, 2)
    total = slot_for(0)
    for k in sends:
        total = total + shift(slot_for(k).astype(BF16), dx=k).astype(F32)
    preact = jnp.maximum(total + up_bias, 0.0)
    gated = preact.reshape(NZ, steps, rows, blocks, -1) * mask[:, :, None, :, None]
    gated = gated.reshape(slot, columns).astype(BF16)

    near = jnp.zeros((NX,) + gated.shape, BF16)
    near = lax.dynamic_update_index_in_dim(near, gated, x, 0)
    for k in sends:
        near = lax.dynamic_update_index_in_dim(near, shift(gated, dx=k), (x - k) % NX, 0)
    other = shift(near, dc=1)

    def out(i):
        own_part = jnp.dot(near[i], down_own, preferred_element_type=F32)
        return own_part + jnp.dot(other[i], down_away, preferred_element_type=F32)

    half = slot // 2
    towards = [(out(1).astype(BF16), -1), (out(2).astype(BF16), 1)]
    early = [shift(part[half:], dy=dy) for part, dy in towards]
    late = [shift(part[:half], dy=dy) for part, dy in towards]

    def sum_z(parts):
        return scatter_z([b for part in parts for b in part.reshape(-1, own_rows, width)])

    crossed = shift(sum_z([out(3)]), dy=2)
    kept = lax.optimization_barrier(out(0))
    late = kept[:half] + late[0].astype(F32) + late[1].astype(F32)
    early = kept[half:] + early[0].astype(F32) + early[1].astype(F32)
    mixed = sum_z([late, early]) + crossed + down_bias.astype(F32)
    return mixed.astype(BF16).reshape(tokens.shape)


def solution(mesh):
    placed = (
        P(None, "dp", "tensor"),
        P("tensor", "dp"),
        P("dp"),
        P("dp", "tensor"),
        P("tensor"),
        P(None, None, "dp"),
    )
    return jax.shard_map(
        local, mesh=mesh, in_specs=placed, out_specs=P(None, "dp", "tensor"), check_vma=False
    )
```

```python
import jax
import jax.numpy as jnp
from jax import lax
from jax.sharding import PartitionSpec as P

AXES = ("dp", "tensor")
NZ, NY, NX, NC = 8, 4, 4, 2
F32 = jnp.float32
BF16 = jnp.bfloat16


def shift(value, dz=0, dy=0, dx=0, dc=0):
    pairs = []
    for z in range(NZ):
        for y in range(NY):
            for x in range(NX):
                for c in range(NC):
                    source = ((z * NY + y) * NX + x) * NC + c
                    zt, yt, xt, ct = (z + dz) % NZ, (y + dy) % NY, (x + dx) % NX, (c + dc) % NC
                    pairs.append((source, ((zt * NY + yt) * NX + xt) * NC + ct))
    return lax.ppermute(value, AXES, pairs)


Z_BLOCKS = (0, 1, -1, 2, -2, 3, -3, 4)


def gather_z(block):
    held = {0: block}
    for k in (1, 2, 3, 4):
        held[k] = shift(held[k - 1], dz=1)
        if k < 4:
            held[-k] = shift(held[1 - k], dz=-1)
    return [held[k] for k in Z_BLOCKS]


def scatter_z(sums):
    part = dict(zip(Z_BLOCKS, sums))
    back, forth = part[4], part[-3]
    for k in (3, 2, 1):
        back = part[k] + shift(back.astype(BF16), dz=-1).astype(F32)
        if k < 3:
            forth = part[-k] + shift(forth.astype(BF16), dz=1).astype(F32)
    return (
        part[0]
        + shift(back.astype(BF16), dz=-1).astype(F32)
        + shift(forth.astype(BF16), dz=1).astype(F32)
    )


def local(tokens, up_weight, up_bias, down_weight, down_bias, active):
    steps, rows, width = tokens.shape
    own_rows = steps * rows
    slot = NZ * own_rows
    hidden_width = up_weight.shape[1]
    columns = hidden_width // NC
    blocks = active.shape[2] // NC
    z = lax.axis_index("dp") // NY
    x = lax.axis_index("tensor") // NC
    c = lax.axis_index("tensor") % NC

    up_own = lax.dynamic_slice_in_dim(up_weight, c * columns, columns, 1)
    up_away = lax.dynamic_slice_in_dim(up_weight, (1 - c) * columns, columns, 1)
    down_own = lax.dynamic_slice_in_dim(down_weight, c * columns, columns, 0)
    down_away = lax.dynamic_slice_in_dim(down_weight, (1 - c) * columns, columns, 0)
    up_bias = lax.dynamic_slice_in_dim(up_bias, c * columns, columns).astype(F32)
    active = lax.dynamic_slice_in_dim(active, c * blocks, blocks, 2).astype(F32)
    row_block = ((z - jnp.asarray(Z_BLOCKS, jnp.int32)) % NZ) // 2
    chosen = (row_block[:, None] == jnp.arange(active.shape[1], dtype=jnp.int32)[None]).astype(F32)
    mask = (chosen[:, None, :, None] * active[None]).sum(2)

    own = tokens.reshape(own_rows, width)
    opposite = shift(own, dy=2)
    col = jnp.concatenate(gather_z(own))
    prev, succ = shift(col, dy=1), shift(col, dy=-1)
    far = jnp.concatenate(gather_z(opposite))
    slots = (col, prev, succ, far)

    away = [shift(jnp.dot(part, up_away, preferred_element_type=F32), dc=1) for part in slots]
    mine = [jnp.dot(part, up_own, preferred_element_type=F32) for part in slots]
    sums = [a + b for a, b in zip(mine, away)]
    rounded = jnp.stack([part.astype(BF16) for part in sums])

    sends = (1, -1, 2)
    total = jnp.where(x < 2, jnp.where(x == 0, sums[0], sums[1]), jnp.where(x == 2, sums[2], sums[3]))
    for k in sends:
        total = total + shift(rounded[(x + k) % NX], dx=k).astype(F32)
    preact = jnp.maximum(total + up_bias, 0.0)
    gated = preact.reshape(NZ, steps, rows, blocks, -1) * mask[:, :, None, :, None]
    gated = lax.optimization_barrier(gated.reshape(slot, columns).astype(BF16))

    near = jnp.zeros((NX,) + gated.shape, BF16)
    near = lax.dynamic_update_index_in_dim(near, gated, x, 0)
    for k in sends:
        near = lax.dynamic_update_index_in_dim(near, shift(gated, dx=k), (x - k) % NX, 0)
    other = shift(near, dc=1)

    partial = jnp.dot(near.reshape(-1, columns), down_own, preferred_element_type=F32)

    def out(i):
        part = jnp.dot(other[i], down_away, preferred_element_type=F32)
        return partial[i * slot : (i + 1) * slot] + part

    back = [shift(out(1).astype(BF16), dy=-1), shift(out(2).astype(BF16), dy=1)]

    def sum_z(part):
        return scatter_z(list(part.reshape(NZ, own_rows, width)))

    crossed = shift(sum_z(out(3)), dy=2)
    summed = out(0) + back[0].astype(F32) + back[1].astype(F32)
    mixed = sum_z(summed) + crossed + down_bias.astype(F32)
    return mixed.astype(BF16).reshape(tokens.shape)


def solution(mesh):
    placed = (
        P(None, "dp", "tensor"),
        P("tensor", "dp"),
        P("dp"),
        P("dp", "tensor"),
        P("tensor"),
        P(None, None, "dp"),
    )
    return jax.shard_map(
        local, mesh=mesh, in_specs=placed, out_specs=P(None, "dp", "tensor"), check_vma=False
    )
```

```python
import jax
import jax.numpy as jnp
from jax import lax
from jax.sharding import PartitionSpec as P

AXES = ("dp", "tensor")
NZ, NY, NX, NC = 8, 4, 4, 2
F32 = jnp.float32
BF16 = jnp.bfloat16


def shift(value, dz=0, dy=0, dx=0, dc=0):
    pairs = []
    for z in range(NZ):
        for y in range(NY):
            for x in range(NX):
                for c in range(NC):
                    source = ((z * NY + y) * NX + x) * NC + c
                    zt, yt, xt, ct = (z + dz) % NZ, (y + dy) % NY, (x + dx) % NX, (c + dc) % NC
                    pairs.append((source, ((zt * NY + yt) * NX + xt) * NC + ct))
    return lax.ppermute(value, AXES, pairs)


Z_BLOCKS = (0, 1, -1, 2, -2, 3, -3, 4)


def gather_z(block):
    held = {0: block}
    for k in (1, 2, 3, 4):
        held[k] = shift(held[k - 1], dz=1)
        if k < 4:
            held[-k] = shift(held[1 - k], dz=-1)
    return [held[k] for k in Z_BLOCKS]


def scatter_z(sums):
    part = dict(zip(Z_BLOCKS, sums))
    back, forth = part[4], part[-3]
    for k in (3, 2, 1):
        back = part[k] + shift(back.astype(BF16), dz=-1).astype(F32)
        if k < 3:
            forth = part[-k] + shift(forth.astype(BF16), dz=1).astype(F32)
    return (
        part[0]
        + shift(back.astype(BF16), dz=-1).astype(F32)
        + shift(forth.astype(BF16), dz=1).astype(F32)
    )


def gather_z_two_rounds(block):
    held = {0: block}
    for k in (1, -1, 2, -2):
        held[k] = shift(block, dz=k)
    more = shift(jnp.concatenate([held[1], held[2]]), dz=2)
    held[3], held[4] = jnp.split(more, 2)
    held[-3] = shift(held[-1], dz=-2)
    return [held[k] for k in Z_BLOCKS]


def scatter_z_two_rounds(sums):
    part = dict(zip(Z_BLOCKS, sums))
    more = shift(jnp.stack([part[3], part[4]]).astype(BF16), dz=-2).astype(F32)
    less = shift(part[-3].astype(BF16), dz=2).astype(F32)
    part[1], part[2], part[-1] = part[1] + more[0], part[2] + more[1], part[-1] + less
    total = part[0]
    for k in (2, -2, 1, -1):
        total = total + shift(part[k].astype(BF16), dz=-k).astype(F32)
    return total


def local(tokens, up_weight, up_bias, down_weight, down_bias, active):
    steps, rows, width = tokens.shape
    own_rows = steps * rows
    slot = NZ * own_rows
    hidden_width = up_weight.shape[1]
    columns = hidden_width // NC
    blocks = active.shape[2] // NC
    z = lax.axis_index("dp") // NY
    x = lax.axis_index("tensor") // NC
    c = lax.axis_index("tensor") % NC

    up_own = lax.dynamic_slice_in_dim(up_weight, c * columns, columns, 1)
    up_away = lax.dynamic_slice_in_dim(up_weight, (1 - c) * columns, columns, 1)
    down_own = lax.dynamic_slice_in_dim(down_weight, c * columns, columns, 0)
    down_away = lax.dynamic_slice_in_dim(down_weight, (1 - c) * columns, columns, 0)
    own = tokens.reshape(own_rows, width)
    opposite = shift(own, dy=2)
    col = jnp.concatenate(gather_z(own))
    col, opposite, active, up_bias = lax.optimization_barrier((col, opposite, active, up_bias))
    prev, succ = shift(col, dy=1), shift(col, dy=-1)
    far = jnp.concatenate(gather_z_two_rounds(opposite))
    up_bias = lax.dynamic_slice_in_dim(up_bias, c * columns, columns).astype(F32)
    active = lax.dynamic_slice_in_dim(active, c * blocks, blocks, 2).astype(F32)
    row_block = ((z - jnp.asarray(Z_BLOCKS, jnp.int32)) % NZ) // 2
    chosen = (row_block[:, None] == jnp.arange(active.shape[1], dtype=jnp.int32)[None]).astype(F32)
    mask = (chosen[:, None, :, None] * active[None]).sum(2)
    slots = (col, prev, succ, far)

    away = [shift(jnp.dot(part, up_away, preferred_element_type=F32), dc=1) for part in slots]
    mine = [jnp.dot(part, up_own, preferred_element_type=F32) for part in slots]
    sums = [a + b for a, b in zip(mine, away)]
    rounded = jnp.stack([part.astype(BF16) for part in sums])

    sends = (1, -1, 2)
    total = jnp.where(x < 2, jnp.where(x == 0, sums[0], sums[1]), jnp.where(x == 2, sums[2], sums[3]))
    for k in sends:
        total = total + shift(rounded[(x + k) % NX], dx=k).astype(F32)
    preact = jnp.maximum(total + up_bias, 0.0)
    gated = preact.reshape(NZ, steps, rows, blocks, -1) * mask[:, :, None, :, None]
    gated = lax.optimization_barrier(gated.reshape(slot, columns).astype(BF16))

    near = jnp.zeros((NX,) + gated.shape, BF16)
    near = lax.dynamic_update_index_in_dim(near, gated, x, 0)
    for k in sends:
        near = lax.dynamic_update_index_in_dim(near, shift(gated, dx=k), (x - k) % NX, 0)
    other = shift(near, dc=1)

    partial = jnp.dot(near.reshape(-1, columns), down_own, preferred_element_type=F32)

    def out(i):
        part = jnp.dot(other[i], down_away, preferred_element_type=F32)
        return partial[i * slot : (i + 1) * slot] + part

    def blocks_of(part):
        return list(part.reshape(NZ, own_rows, width))

    across = scatter_z_two_rounds(blocks_of(out(3)))
    back = [shift(out(1).astype(BF16), dy=-1), shift(out(2).astype(BF16), dy=1)]
    summed = out(0) + back[0].astype(F32) + back[1].astype(F32)
    summed, across = lax.optimization_barrier((summed, across))
    crossed = shift(across, dy=2)
    mixed = scatter_z(blocks_of(summed)) + crossed + down_bias.astype(F32)
    return mixed.astype(BF16).reshape(tokens.shape)


def solution(mesh):
    placed = (
        P(None, "dp", "tensor"),
        P("tensor", "dp"),
        P("dp"),
        P("dp", "tensor"),
        P("tensor"),
        P(None, None, "dp"),
    )
    return jax.shard_map(
        local, mesh=mesh, in_specs=placed, out_specs=P(None, "dp", "tensor"), check_vma=False
    )
```

```python
import jax
import jax.numpy as jnp
from jax import lax
from jax.sharding import PartitionSpec as P

AXES = ("dp", "tensor")
NZ, NY, NX, NC = 8, 4, 4, 2
F32 = jnp.float32
BF16 = jnp.bfloat16


def shift(value, dz=0, dy=0, dx=0, dc=0):
    pairs = []
    for z in range(NZ):
        for y in range(NY):
            for x in range(NX):
                for c in range(NC):
                    source = ((z * NY + y) * NX + x) * NC + c
                    zt, yt, xt, ct = (z + dz) % NZ, (y + dy) % NY, (x + dx) % NX, (c + dc) % NC
                    pairs.append((source, ((zt * NY + yt) * NX + xt) * NC + ct))
    return lax.ppermute(value, AXES, pairs)


Z_BLOCKS = (0, 1, -1, 2, -2, 3, -3, 4)


def gather_z(block):
    held = {0: block}
    for k in (1, -1, 2, -2):
        held[k] = shift(block, dz=k)
    more = shift(jnp.concatenate([held[1], held[2]]), dz=2)
    held[3], held[4] = jnp.split(more, 2)
    held[-3] = shift(held[-1], dz=-2)
    return [held[k] for k in Z_BLOCKS]


def scatter_z(sums):
    part = dict(zip(Z_BLOCKS, sums))
    more = shift(jnp.stack([part[3], part[4]]).astype(BF16), dz=-2).astype(F32)
    less = shift(part[-3].astype(BF16), dz=2).astype(F32)
    part[1], part[2], part[-1] = part[1] + more[0], part[2] + more[1], part[-1] + less
    total = part[0]
    for k in (2, -2, 1, -1):
        total = total + shift(part[k].astype(BF16), dz=-k).astype(F32)
    return total


def local(tokens, up_weight, up_bias, down_weight, down_bias, active):
    steps, rows, width = tokens.shape
    own_rows = steps * rows
    slot = NZ * own_rows
    hidden_width = up_weight.shape[1]
    columns = hidden_width // NC
    blocks = active.shape[2] // NC
    z = lax.axis_index("dp") // NY
    x = lax.axis_index("tensor") // NC
    c = lax.axis_index("tensor") % NC

    up_own = lax.dynamic_slice_in_dim(up_weight, c * columns, columns, 1)
    up_away = lax.dynamic_slice_in_dim(up_weight, (1 - c) * columns, columns, 1)
    down_own = lax.dynamic_slice_in_dim(down_weight, c * columns, columns, 0)
    down_away = lax.dynamic_slice_in_dim(down_weight, (1 - c) * columns, columns, 0)
    own = tokens.reshape(own_rows, width)
    opposite = shift(own, dy=2)
    col = jnp.concatenate(gather_z(own))
    col, opposite, active, up_bias = lax.optimization_barrier((col, opposite, active, up_bias))
    prev, succ = shift(col, dy=1), shift(col, dy=-1)
    far = jnp.concatenate(gather_z(opposite))
    up_bias = lax.dynamic_slice_in_dim(up_bias, c * columns, columns).astype(F32)
    active = lax.dynamic_slice_in_dim(active, c * blocks, blocks, 2).astype(F32)
    row_block = ((z - jnp.asarray(Z_BLOCKS, jnp.int32)) % NZ) // 2
    chosen = (row_block[:, None] == jnp.arange(active.shape[1], dtype=jnp.int32)[None]).astype(F32)
    mask = (chosen[:, None, :, None] * active[None]).sum(2)
    slots = (col, prev, succ, far)

    away = [shift(jnp.dot(part, up_away, preferred_element_type=F32), dc=1) for part in slots]
    mine = [jnp.dot(part, up_own, preferred_element_type=F32) for part in slots]
    sums = [a + b for a, b in zip(mine, away)]
    rounded = jnp.stack([part.astype(BF16) for part in sums])

    sends = (1, -1, 2)
    total = jnp.where(x < 2, jnp.where(x == 0, sums[0], sums[1]), jnp.where(x == 2, sums[2], sums[3]))
    for k in sends:
        total = total + shift(rounded[(x + k) % NX], dx=k).astype(F32)
    preact = jnp.maximum(total + up_bias, 0.0)
    gated = preact.reshape(NZ, steps, rows, blocks, -1) * mask[:, :, None, :, None]
    gated = lax.optimization_barrier(gated.reshape(slot, columns).astype(BF16))

    near = jnp.zeros((NX,) + gated.shape, BF16)
    near = lax.dynamic_update_index_in_dim(near, gated, x, 0)
    for k in sends:
        near = lax.dynamic_update_index_in_dim(near, shift(gated, dx=k), (x - k) % NX, 0)
    other = shift(near, dc=1)

    partial = jnp.dot(near.reshape(-1, columns), down_own, preferred_element_type=F32)

    def out(i):
        part = jnp.dot(other[i], down_away, preferred_element_type=F32)
        return partial[i * slot : (i + 1) * slot] + part

    def blocks_of(part):
        return list(part.reshape(NZ, own_rows, width))

    before, after = out(1).astype(BF16), out(2).astype(BF16)
    before, after, other = lax.optimization_barrier((before, after, other))
    back = [shift(before, dy=-1), shift(after, dy=1)]
    across = scatter_z(blocks_of(out(3)))
    summed = out(0) + back[0].astype(F32) + back[1].astype(F32)
    summed, across = lax.optimization_barrier((summed, across))
    crossed = shift(across, dy=2)
    mixed = scatter_z(blocks_of(summed)) + crossed + down_bias.astype(F32)
    return mixed.astype(BF16).reshape(tokens.shape)


def solution(mesh):
    placed = (
        P(None, "dp", "tensor"),
        P("tensor", "dp"),
        P("dp"),
        P("dp", "tensor"),
        P("tensor"),
        P(None, None, "dp"),
    )
    return jax.shard_map(
        local, mesh=mesh, in_specs=placed, out_specs=P(None, "dp", "tensor"), check_vma=False
    )
```

```python
import jax
import jax.numpy as jnp
from jax import lax
from jax.sharding import PartitionSpec as P

AXES = ("dp", "tensor")
NZ, NY, NX, NC = 8, 4, 4, 2
F32 = jnp.float32
BF16 = jnp.bfloat16


def shift(value, dz=0, dy=0, dx=0, dc=0):
    pairs = []
    for z in range(NZ):
        for y in range(NY):
            for x in range(NX):
                for c in range(NC):
                    source = ((z * NY + y) * NX + x) * NC + c
                    zt, yt, xt, ct = (z + dz) % NZ, (y + dy) % NY, (x + dx) % NX, (c + dc) % NC
                    pairs.append((source, ((zt * NY + yt) * NX + xt) * NC + ct))
    return lax.ppermute(value, AXES, pairs)


Z_BLOCKS = (0, 1, -1, 2, -2, 3, -3, 4)


def gather_z(block):
    held = {0: block}
    for k in (1, -1, 2, -2):
        held[k] = shift(block, dz=k)
    more = shift(jnp.concatenate([held[1], held[2]]), dz=2)
    held[3], held[4] = jnp.split(more, 2)
    held[-3] = shift(held[-1], dz=-2)
    return [held[k] for k in Z_BLOCKS]


def scatter_z(sums):
    part = dict(zip(Z_BLOCKS, sums))
    more = shift(jnp.stack([part[3], part[4]]).astype(BF16), dz=-2).astype(F32)
    less = shift(part[-3].astype(BF16), dz=2).astype(F32)
    part[1], part[2], part[-1] = part[1] + more[0], part[2] + more[1], part[-1] + less
    total = part[0]
    for k in (2, -2, 1, -1):
        total = total + shift(part[k].astype(BF16), dz=-k).astype(F32)
    return total


def local(tokens, up_weight, up_bias, down_weight, down_bias, active):
    steps, rows, width = tokens.shape
    own_rows = steps * rows
    slot = NZ * own_rows
    hidden_width = up_weight.shape[1]
    columns = hidden_width // NC
    blocks = active.shape[2] // NC
    z = lax.axis_index("dp") // NY
    x = lax.axis_index("tensor") // NC
    c = lax.axis_index("tensor") % NC

    up_own = lax.dynamic_slice_in_dim(up_weight, c * columns, columns, 1)
    up_away = lax.dynamic_slice_in_dim(up_weight, (1 - c) * columns, columns, 1)
    down_own = lax.dynamic_slice_in_dim(down_weight, c * columns, columns, 0)
    down_away = lax.dynamic_slice_in_dim(down_weight, (1 - c) * columns, columns, 0)
    own = tokens.reshape(own_rows, width)
    opposite = shift(own, dy=2)
    col = jnp.concatenate(gather_z(own))
    col = lax.optimization_barrier(col)
    prev, succ = shift(col, dy=1), shift(col, dy=-1)
    col_away = jnp.dot(col, up_away, preferred_element_type=F32)
    col_away, opposite, active, up_bias = lax.optimization_barrier((col_away, opposite, active, up_bias))
    far = jnp.concatenate(gather_z(opposite))
    up_bias = lax.dynamic_slice_in_dim(up_bias, c * columns, columns).astype(F32)
    active = lax.dynamic_slice_in_dim(active, c * blocks, blocks, 2).astype(F32)
    row_block = ((z - jnp.asarray(Z_BLOCKS, jnp.int32)) % NZ) // 2
    chosen = (row_block[:, None] == jnp.arange(active.shape[1], dtype=jnp.int32)[None]).astype(F32)
    mask = (chosen[:, None, :, None] * active[None]).sum(2)
    slots = (col, prev, succ, far)

    away = [shift(col_away, dc=1)] + [
        shift(jnp.dot(part, up_away, preferred_element_type=F32), dc=1) for part in slots[1:]
    ]
    mine = [jnp.dot(part, up_own, preferred_element_type=F32) for part in slots]
    sums = [a + b for a, b in zip(mine, away)]
    rounded = jnp.stack([part.astype(BF16) for part in sums])

    sends = (1, -1, 2)
    total = jnp.where(x < 2, jnp.where(x == 0, sums[0], sums[1]), jnp.where(x == 2, sums[2], sums[3]))
    for k in sends:
        total = total + shift(rounded[(x + k) % NX], dx=k).astype(F32)
    preact = jnp.maximum(total + up_bias, 0.0)
    gated = preact.reshape(NZ, steps, rows, blocks, -1) * mask[:, :, None, :, None]
    gated = lax.optimization_barrier(gated.reshape(slot, columns).astype(BF16))

    near = jnp.zeros((NX,) + gated.shape, BF16)
    near = lax.dynamic_update_index_in_dim(near, gated, x, 0)
    for k in sends:
        near = lax.dynamic_update_index_in_dim(near, shift(gated, dx=k), (x - k) % NX, 0)
    other = shift(near, dc=1)

    partial = jnp.dot(near.reshape(-1, columns), down_own, preferred_element_type=F32)

    def out(i):
        part = jnp.dot(other[i], down_away, preferred_element_type=F32)
        return partial[i * slot : (i + 1) * slot] + part

    def blocks_of(part):
        return list(part.reshape(NZ, own_rows, width))

    before, after = out(1).astype(BF16), out(2).astype(BF16)
    before, after, other = lax.optimization_barrier((before, after, other))
    back = [shift(before, dy=-1), shift(after, dy=1)]
    across = scatter_z(blocks_of(out(3)))
    summed = out(0) + back[0].astype(F32) + back[1].astype(F32)
    summed, across = lax.optimization_barrier((summed, across))
    crossed = shift(across, dy=2)
    mixed = scatter_z(blocks_of(summed)) + crossed + down_bias.astype(F32)
    return mixed.astype(BF16).reshape(tokens.shape)


def solution(mesh):
    placed = (
        P(None, "dp", "tensor"),
        P("tensor", "dp"),
        P("dp"),
        P("dp", "tensor"),
        P("tensor"),
        P(None, None, "dp"),
    )
    return jax.shard_map(
        local, mesh=mesh, in_specs=placed, out_specs=P(None, "dp", "tensor"), check_vma=False
    )
```

```python
import jax
import jax.numpy as jnp
from jax import lax
from jax.sharding import PartitionSpec as P

AXES = ("dp", "tensor")
NZ, NY, NX, NC = 8, 4, 4, 2
F32 = jnp.float32
BF16 = jnp.bfloat16


def shift(value, dz=0, dy=0, dx=0, dc=0):
    pairs = []
    for z in range(NZ):
        for y in range(NY):
            for x in range(NX):
                for c in range(NC):
                    source = ((z * NY + y) * NX + x) * NC + c
                    zt, yt, xt, ct = (z + dz) % NZ, (y + dy) % NY, (x + dx) % NX, (c + dc) % NC
                    pairs.append((source, ((zt * NY + yt) * NX + xt) * NC + ct))
    return lax.ppermute(value, AXES, pairs)


Z_BLOCKS = (0, 1, -1, 2, -2, 3, -3, 4)


def gather_z(block):
    held = {0: block}
    for k in (1, -1, 2, -2):
        held[k] = shift(block, dz=k)
    more = shift(jnp.concatenate([held[1], held[2]]), dz=2)
    held[3], held[4] = jnp.split(more, 2)
    held[-3] = shift(held[-1], dz=-2)
    return [held[k] for k in Z_BLOCKS]


def scatter_z(sums):
    part = dict(zip(Z_BLOCKS, sums))
    more = shift(jnp.stack([part[3], part[4]]).astype(BF16), dz=-2).astype(F32)
    less = shift(part[-3].astype(BF16), dz=2).astype(F32)
    part[1], part[2], part[-1] = part[1] + more[0], part[2] + more[1], part[-1] + less
    total = part[0]
    for k in (2, -2, 1, -1):
        total = total + shift(part[k].astype(BF16), dz=-k).astype(F32)
    return total


def local(tokens, up_weight, up_bias, down_weight, down_bias, active):
    steps, rows, width = tokens.shape
    own_rows = steps * rows
    slot = NZ * own_rows
    hidden_width = up_weight.shape[1]
    columns = hidden_width // NC
    blocks = active.shape[2] // NC
    z = lax.axis_index("dp") // NY
    x = lax.axis_index("tensor") // NC
    c = lax.axis_index("tensor") % NC

    up_own = lax.dynamic_slice_in_dim(up_weight, c * columns, columns, 1)
    up_away = lax.dynamic_slice_in_dim(up_weight, (1 - c) * columns, columns, 1)
    down_own = lax.dynamic_slice_in_dim(down_weight, c * columns, columns, 0)
    down_away = lax.dynamic_slice_in_dim(down_weight, (1 - c) * columns, columns, 0)
    own = tokens.reshape(own_rows, width)
    opposite = shift(own, dy=2)
    col = jnp.concatenate(gather_z(own))
    col = lax.optimization_barrier(col)
    prev, succ = shift(col, dy=1), shift(col, dy=-1)
    col_away = jnp.dot(col, up_away, preferred_element_type=F32)
    col_away, opposite, active, up_bias = lax.optimization_barrier((col_away, opposite, active, up_bias))
    far = jnp.concatenate(gather_z(opposite))
    up_bias = lax.dynamic_slice_in_dim(up_bias, c * columns, columns).astype(F32)
    active = lax.dynamic_slice_in_dim(active, c * blocks, blocks, 2).astype(F32)
    row_block = ((z - jnp.asarray(Z_BLOCKS, jnp.int32)) % NZ) // 2
    chosen = (row_block[:, None] == jnp.arange(active.shape[1], dtype=jnp.int32)[None]).astype(F32)
    mask = (chosen[:, None, :, None] * active[None]).sum(2)
    slots = (col, prev, succ, far)

    away = [shift(col_away, dc=1)] + [
        shift(jnp.dot(part, up_away, preferred_element_type=F32), dc=1) for part in slots[1:]
    ]
    mine = [jnp.dot(part, up_own, preferred_element_type=F32) for part in slots]
    sums = [a + b for a, b in zip(mine, away)]
    rounded = jnp.stack([part.astype(BF16) for part in sums])

    sends = (1, -1, 2)
    total = jnp.where(x < 2, jnp.where(x == 0, sums[0], sums[1]), jnp.where(x == 2, sums[2], sums[3]))
    for k in sends:
        total = total + shift(rounded[(x + k) % NX], dx=k).astype(F32)
    preact = jnp.maximum(total + up_bias, 0.0)
    gated = preact.reshape(NZ, steps, rows, blocks, -1) * mask[:, :, None, :, None]
    gated = lax.optimization_barrier(gated.reshape(slot, columns).astype(BF16))

    near = jnp.zeros((NX,) + gated.shape, BF16)
    near = lax.dynamic_update_index_in_dim(near, gated, x, 0)
    for k in sends:
        near = lax.dynamic_update_index_in_dim(near, shift(gated, dx=k), (x - k) % NX, 0)
    other = shift(near, dc=1)

    partial = jnp.dot(near.reshape(-1, columns), down_own, preferred_element_type=F32)

    def out(i):
        part = jnp.dot(other[i], down_away, preferred_element_type=F32)
        return partial[i * slot : (i + 1) * slot] + part

    def blocks_of(part):
        return list(part.reshape(NZ, own_rows, width))

    before, after = out(1).astype(BF16), out(2).astype(BF16)
    before, after, other = lax.optimization_barrier((before, after, other))
    back = [shift(before, dy=-1), shift(after, dy=1)]
    kept, distant = lax.optimization_barrier((out(0), out(3)))
    across = scatter_z(blocks_of(distant))
    summed = kept + back[0].astype(F32) + back[1].astype(F32)
    summed, across = lax.optimization_barrier((summed, across))
    crossed = shift(across, dy=2)
    mixed = scatter_z(blocks_of(summed)) + crossed + down_bias.astype(F32)
    return mixed.astype(BF16).reshape(tokens.shape)


def solution(mesh):
    placed = (
        P(None, "dp", "tensor"),
        P("tensor", "dp"),
        P("dp"),
        P("dp", "tensor"),
        P("tensor"),
        P(None, None, "dp"),
    )
    return jax.shard_map(
        local, mesh=mesh, in_specs=placed, out_specs=P(None, "dp", "tensor"), check_vma=False
    )
```
